256 devices in a mesh: blk: 64 (over y, z, core), rep: 4 (over x).
Axes of the slice: x: 4, y: 4, z: 8, core: 2. Of those that a mesh axis runs over, the one named last changes fastest.
Arguments:
- embeddings: bfloat16 [98304, 1024], P('blk'), may hold values from -12 to 12
- pick: int32 [64, 64], replicated, may hold values from 0 to 6, as said below
- mask: int32 [64, 64, 6], replicated, may hold values from 0 to 1, as said below
Outputs:
- log_weight: float32 [384, 256], P('blk', 'rep')
The draws below stay inside these ranges and needn't reach their ends.
Inputs may be any that keep to these rules, and one draw needn't show every extreme that they name: pick[k, k] = 6; a value of 6 means that owner k takes no block of owner p. mask[k, p, a] is 0 wherever pick[k, p] = 6, and is 1 for at least one a wherever pick[k, p] < 6.
All inputs are finite; a program needn't handle non-finite values.
Results may differ from the reference program's by a relative error of at most 0.0003.
Values may be sent and summed in bfloat16 or wider, within the bound.
A program may use at most 384 MiB of HBM per device.

```python
import math
import jax
import jax.numpy as jnp
from jax import lax

W = 1024
BR = 256
BLK_DEV = 6
N_BLK = 64


def pick_table(key):
    key_rate, key_take, key_one, key_two = jax.random.split(key, 4)
    take_rate = jax.random.randint(key_rate, (N_BLK, 1), 3, 10)
    is_taken = jax.random.randint(key_take, (N_BLK, N_BLK), 0, 10) < take_rate
    first_pick = jax.random.randint(key_one, (N_BLK, N_BLK), 0, BLK_DEV)
    second_pick = jax.random.randint(key_two, (N_BLK, N_BLK), 0, BLK_DEV)
    diagonal = jnp.arange(N_BLK)[:, None] == jnp.arange(N_BLK)[None, :]
    is_taken = is_taken & jnp.logical_not(diagonal)
    return jnp.where(is_taken, jnp.minimum(first_pick, second_pick), BLK_DEV).astype(jnp.int32)


def draw_pick(key, part):
    return pick_table(key)


def draw_mask(key, part):
    pick_values = pick_table(key)
    key = jax.random.fold_in(key, 7)
    extra_bits = jax.random.randint(key, (N_BLK, N_BLK, BLK_DEV), 0, 4) != 0
    lane_index = jnp.arange(BLK_DEV)[None, None, :]
    forced = lane_index == ((jnp.arange(N_BLK)[:, None] + jnp.arange(N_BLK)[None, :]) % BLK_DEV)[:, :, None]
    is_paired = (pick_values < BLK_DEV)[:, :, None] & (extra_bits | forced)
    return is_paired.astype(jnp.int32)


def draw_embeddings(key, part):
    key = jax.random.fold_in(key, 3)
    key_scale, key_body = jax.random.split(key, 2)
    row_count = N_BLK * BLK_DEV * BR
    spread = jnp.exp(jax.random.uniform(key_scale, (row_count, 1), minval=math.log(0.5), maxval=math.log(2.0)))
    values = spread * jax.random.normal(key_body, (row_count, W))
    return jnp.clip(values, -12.0, 12.0).astype(jnp.bfloat16)


def setup_inputs(seed: int = 0) -> dict:
    key_list = jax.random.split(jax.random.key(seed), 4)
    embeddings = draw_embeddings(jax.random.fold_in(key_list[3], 71), 0)
    pick = draw_pick(jax.random.fold_in(key_list[3], 71), 0)
    mask = draw_mask(jax.random.fold_in(key_list[3], 71), 0)
    return {"embeddings": embeddings, "pick": pick, "mask": mask}


MIN_SCORE = -1e+30

def combine_pair(peak_a, total_a, peak_b, total_b):
    peak_new = jnp.maximum(peak_a, peak_b)
    return (peak_new, total_a * jnp.exp(peak_a - peak_new) + total_b * jnp.exp(peak_b - peak_new))

def reference(embeddings, pick, mask):
    blocks = embeddings.reshape(N_BLK * BLK_DEV, BR, W)
    score_scale = 1.0 / math.sqrt(W)
    self_mask = jnp.arange(BR)[:, None] == jnp.arange(BR)[None, :]

    def own_stats(block):
        scores = jnp.dot(block, block.T, preferred_element_type=jnp.float32) * score_scale
        scores = jnp.where(self_mask, MIN_SCORE, scores)
        row_peak = lax.optimization_barrier(jnp.max(scores, axis=1))
        return (row_peak, lax.optimization_barrier(jnp.sum(jnp.exp(scores - row_peak[:, None]), axis=1)))
    peak_table, totals = lax.map(own_stats, blocks)

    def absorb_pair(state_now, item_index):
        requester = item_index // (N_BLK * BLK_DEV)
        owner_id = item_index // BLK_DEV % N_BLK
        local_id = item_index % BLK_DEV
        chosen = pick[requester, owner_id]
        is_live = (chosen < BLK_DEV) & (mask[requester, owner_id, local_id] == 1)

        def update(state_in):
            peaks_in, totals_in = state_in
            left_id = (requester * BLK_DEV + local_id).astype(jnp.int32)
            right_id = (owner_id * BLK_DEV + jnp.minimum(chosen, BLK_DEV - 1)).astype(jnp.int32)
            left_block = blocks[left_id]
            right_block = blocks[right_id]
            scores = jnp.dot(left_block, right_block.T, preferred_element_type=jnp.float32) * score_scale
            row_peak = lax.optimization_barrier(jnp.max(scores, axis=1))
            row_total = lax.optimization_barrier(jnp.sum(jnp.exp(scores - row_peak[:, None]), axis=1))
            col_peak = lax.optimization_barrier(jnp.max(scores, axis=0))
            col_total = lax.optimization_barrier(jnp.sum(jnp.exp(scores - col_peak[None, :]), axis=0))
            new_peak, new_total = combine_pair(peaks_in[left_id], totals_in[left_id], row_peak, row_total)
            peaks_in = peaks_in.at[left_id].set(new_peak)
            totals_in = totals_in.at[left_id].set(new_total)
            new_peak, new_total = combine_pair(peaks_in[right_id], totals_in[right_id], col_peak, col_total)
            peaks_in = peaks_in.at[right_id].set(new_peak)
            totals_in = totals_in.at[right_id].set(new_total)
            return (peaks_in, totals_in)

        def unchanged(state_in):
            return state_in
        return (lax.cond(is_live, update, unchanged, state_now), None)
    item_list = jnp.arange(N_BLK * N_BLK * BLK_DEV, dtype=jnp.int32)
    (peak_table, totals), _ = lax.scan(absorb_pair, (peak_table, totals), item_list)
    return peak_table + jnp.log(totals)
```

```python
import math

import jax
import jax.numpy as jnp
from jax import lax
from jax.experimental import pallas as pl
from jax.experimental.pallas import tpu as pltpu
from jax.sharding import PartitionSpec as P

W = 1024
BR = 256
BLK_DEV = 6
NY, NZ, NC, NX = 4, 8, 2, 4
PLANE = NY * NC
Q = BR // NX
COLS = PLANE * Q
SLOTS = NZ
LOW = -1e30
TO_BASE2 = math.log2(math.e) / math.sqrt(W)
LN2 = math.log(2.0)
NT = (((1,), (1,)), ((), ()))


def kernel(
    emb, pick, bias, pcol, out,
    q0, ra1, ra2, ra3, rb1, rb2, rb3, r4, staged, held, row_max, row_sum, col_max, col_sum,
    col_send, col_mid, col_turn, col_got, row_send, row_got,
    z_send, z_recv, y_send, y_recv, cy_send, cy_recv, cz_send, cz_recv, x_send, x_recv,
):
    me = lax.axis_index("blk")
    x = lax.axis_index("rep")
    c = lax.rem(me, NC)
    z = lax.rem(me // NC, NZ)
    y = me // (NC * NZ)

    def blk_id(yy, zz, cc):
        return (yy * NZ + zz) * NC + cc

    def z_peer(dz):
        return blk_id(y, lax.rem(z + dz + NZ, NZ), c)

    def plane_peer(j):
        return lax.rem(y + j // NC, NY), lax.rem(c + j % NC, NC)

    def send(src, dst, ssem, rsem, target):
        copy = pltpu.make_async_remote_copy(
            src_ref=src, dst_ref=dst, send_sem=ssem, recv_sem=rsem,
            device_id=target, device_id_type=pl.DeviceIdType.MESH,
        )
        copy.start()
        return copy

    barrier = pltpu.get_barrier_semaphore()
    for dz in range(1, NZ):
        pl.semaphore_signal(barrier, inc=1, device_id={"blk": z_peer(dz)}, device_id_type=pl.DeviceIdType.MESH)
    for j in range(1, PLANE):
        yy, cc = plane_peer(j)
        pl.semaphore_signal(barrier, inc=1, device_id={"blk": blk_id(yy, z, cc)}, device_id_type=pl.DeviceIdType.MESH)
    for dx in range(1, NX):
        pl.semaphore_signal(barrier, inc=1, device_id={"rep": lax.rem(x + dx, NX)}, device_id_type=pl.DeviceIdType.MESH)

    for a in range(BLK_DEV):
        q0[a] = emb[pl.ds(a * BR + x * Q, Q), :]
    pl.semaphore_wait(barrier, NZ - 1 + PLANE - 1 + NX - 1)

    pending = []
    ring_a = [q0, ra1, ra2, ra3]
    ring_b = [q0, rb1, rb2, rb3]
    right, left = {"blk": z_peer(1)}, {"blk": z_peer(-1)}
    half = BLK_DEV // 2

    def push_ring(d):
        if d < 3:
            a = send(ring_a[d], ring_a[d + 1], z_send.at[0, d], z_recv.at[0, d], right)
            b = send(ring_b[d], ring_b[d + 1], z_send.at[1, d], z_recv.at[1, d], left)
        else:
            a = send(ring_a[3].at[pl.ds(0, half)], r4.at[pl.ds(0, half)], z_send.at[0, 3], z_recv.at[0, 3], right)
            b = send(ring_b[3].at[pl.ds(half, half)], r4.at[pl.ds(half, half)], z_send.at[1, 3], z_recv.at[1, 3], left)
        pending.extend([a, b])
        return a, b

    plane_copies = {}

    def stage(slot, ring_ref, zz):
        owner = blk_id(y, zz, c)
        for j in [*range(1, PLANE), 0]:
            yy, cc = plane_peer(j)
            chosen = jnp.clip(pick[blk_id(yy, z, cc), owner], 0, BLK_DEV - 1)
            rows = ring_ref[chosen]
            if j == 0:
                held[zz, y * NC + c] = rows
            else:
                staged[slot, j - 1] = rows
                copy = send(
                    staged.at[slot, j - 1], held.at[zz, y * NC + c],
                    y_send.at[slot, j - 1], y_recv.at[slot, j - 1], {"blk": blk_id(yy, z, cc)},
                )
                plane_copies[slot, j] = copy
                pending.append(copy)

    def own_block(a, carry):
        base = pl.multiple_of(a * BR, BR)
        top = pl.multiple_of((x // 2) * (2 * Q), 2 * Q)
        scores = lax.dot_general(
            emb[pl.ds(base, BR), :], emb[pl.ds(base + top, 2 * Q), :], NT,
            preferred_element_type=jnp.float32,
        ) * TO_BASE2
        row = lax.broadcasted_iota(jnp.int32, (BR, 2 * Q), 0)
        col = lax.broadcasted_iota(jnp.int32, (BR, 2 * Q), 1) + top
        valid = (col // Q == x) & (row != col)
        row_max[a] = jnp.where(valid, scores, LOW)
        row_sum[a] = jnp.where(valid, 1.0, 0.0)
        return carry

    def compute(slot, zz):
        for j in range(1, PLANE):
            plane_copies[slot, j].wait_recv()
        col_max[...] = jnp.full_like(col_max, LOW)
        col_sum[...] = jnp.zeros_like(col_sum)

        def one(a, carry):
            base = pl.multiple_of(a * BR, BR)
            t = lax.dot_general(
                emb[pl.ds(base, BR), :], held[zz].reshape(COLS, W), NT,
                preferred_element_type=jnp.float32,
            ) * TO_BASE2 + bias[zz, a]
            parts = [t[:, g * 128:(g + 1) * 128] for g in range(COLS // 128)]
            old = row_max[a]
            new = old
            for part in parts:
                new = jnp.maximum(new, part)
            total = row_sum[a] * jnp.exp2(old - new)
            for part in parts:
                total += jnp.exp2(part - new)
            row_max[a] = new
            row_sum[a] = total
            t8 = t.reshape(BR // 8, 8, COLS)
            old = col_max[...]
            new = jnp.maximum(old, jnp.max(t8, axis=0))
            col_sum[...] = col_sum[...] * jnp.exp2(old - new) + jnp.sum(jnp.exp2(t8 - new[None]), axis=0)
            col_max[...] = new
            return carry

        lax.fori_loop(0, BLK_DEV, one, 0)
        peak = jnp.max(col_max[...], axis=0, keepdims=True)
        total = jnp.sum(col_sum[...] * jnp.exp2(col_max[...] - peak), axis=0, keepdims=True)
        lse = peak + jnp.log2(total)
        for yy in range(NY):
            col_send[yy, pl.ds(zz, 1), :] = lse[:, yy * 128:(yy + 1) * 128]

    def zat(dz):
        return lax.rem(z + dz + NZ, NZ)

    ring = push_ring(0)
    stage(0, q0, z)
    lax.fori_loop(0, BLK_DEV, own_block, 0)
    ready = [(0, z)]
    for d in range(1, 4):
        ring[0].wait_recv()
        ring[1].wait_recv()
        ring = push_ring(d)
        stage(2 * d - 1, ring_a[d], zat(-d))
        stage(2 * d, ring_b[d], zat(d))
        for slot, zz in ready:
            compute(slot, zz)
        ready = [(2 * d - 1, zat(-d)), (2 * d, zat(d))]
    ring[0].wait_recv()
    ring[1].wait_recv()
    stage(7, r4, zat(4))
    for slot, zz in [*ready, (7, zat(4))]:
        compute(slot, zz)

    back = []
    for j in range(1, PLANE):
        yy, cc = plane_peer(j)
        back.append(send(
            col_send.at[yy], col_mid.at[y * NC + c], cy_send.at[j - 1], cy_recv.at[j - 1],
            {"blk": blk_id(yy, z, cc)},
        ))
    col_mid[y * NC + c] = col_send[y]

    row_send[...] = jnp.full_like(row_send, LOW)
    for a in range(BLK_DEV):
        m = row_max[a].T
        s = row_sum[a].T
        peak = jnp.max(m, axis=0, keepdims=True)
        lse = peak + jnp.log2(jnp.sum(s * jnp.exp2(m - peak), axis=0, keepdims=True))
        for h in range(2):
            row_send[h, a:a + 1, :] = lse[:, h * 128:(h + 1) * 128]
    across = []
    for dx in range(1, NX):
        xx = lax.rem(x + dx, NX)
        across.append(send(row_send.at[xx // 2], row_got.at[x], x_send.at[dx - 1], x_recv.at[dx - 1], {"rep": xx}))
    row_got[x] = row_send[x // 2]

    for copy in back:
        copy.wait_recv()
    for zz in range(NZ):
        for s in range(PLANE):
            col_turn[zz, s:s + 1, :] = col_mid[s, zz:zz + 1, :]
    final = []
    for dz in range(1, NZ):
        zz = zat(dz)
        final.append(send(
            col_turn.at[zz], col_got.at[z], cz_send.at[dz - 1], cz_recv.at[dz - 1], {"blk": blk_id(y, zz, c)}
        ))
    col_got[z] = col_turn[z]
    for copy in across:
        copy.wait_recv()
    for copy in final:
        copy.wait_recv()

    def to_front(v, shift_it):
        return jnp.where(shift_it, pltpu.roll(v, 64, 1), v)

    got = col_got[...].reshape(NZ * PLANE, 128)
    who = pcol[...].reshape(NZ * PLANE, 128)
    for b in range(BLK_DEV):
        chosen = who == b
        v = jnp.where(chosen, got, LOW)
        peak = jnp.max(v, axis=0, keepdims=True)
        total = jnp.sum(jnp.where(chosen, jnp.exp2(v - peak), 0.0), axis=0, keepdims=True)
        col_max[b:b + 1, 0:128] = peak
        col_sum[b:b + 1, 0:128] = total
    col_peak = to_front(col_max[:, 0:128], c == 1)
    col_total = to_front(col_sum[:, 0:128], c == 1)
    rows = [to_front(row_got[i], lax.rem(x, 2) == 1) for i in range(NX)]
    peak = col_peak
    for r in rows:
        peak = jnp.maximum(peak, r)
    total = col_total * jnp.exp2(col_peak - peak)
    for r in rows:
        total += jnp.exp2(r - peak)
    result = (peak + jnp.log2(total)) * LN2
    out[...] = result[:BLK_DEV, :Q]
    for copy in [*pending, *back, *across, *final]:
        copy.wait_send()


def body(embeddings, pick, mask):
    me = lax.axis_index("blk")
    live = mask[me].reshape(NY, NZ, NC, BLK_DEV).transpose(1, 3, 0, 2)
    bias = jnp.where(live == 1, 0.0, LOW).astype(jnp.float32)
    bias = jnp.broadcast_to(bias[..., None], (NZ, BLK_DEV, NY, NC, Q)).reshape(NZ, BLK_DEV, 1, COLS)
    pcol = pick[:, me].reshape(NY, NZ, NC).transpose(1, 0, 2).reshape(NZ, PLANE, 1)
    pcol = jnp.broadcast_to(pcol, (NZ, PLANE, 128))
    vmem = pl.BlockSpec(memory_space=pltpu.VMEM)
    dma = pltpu.SemaphoreType.DMA
    slab = pltpu.VMEM((BLK_DEV, Q, W), jnp.bfloat16)
    f32 = jnp.float32
    return pl.pallas_call(
        kernel,
        out_shape=jax.ShapeDtypeStruct((BLK_DEV, Q), f32),
        in_specs=[vmem, pl.BlockSpec(memory_space=pltpu.SMEM), vmem, vmem],
        out_specs=vmem,
        scratch_shapes=[
            *[slab] * 8,
            pltpu.VMEM((SLOTS, PLANE - 1, Q, W), jnp.bfloat16),
            pltpu.VMEM((NZ, PLANE, Q, W), jnp.bfloat16),
            pltpu.VMEM((BLK_DEV, BR, 128), f32),
            pltpu.VMEM((BLK_DEV, BR, 128), f32),
            pltpu.VMEM((8, COLS), f32),
            pltpu.VMEM((8, COLS), f32),
            pltpu.VMEM((NY, NZ, 128), f32),
            pltpu.VMEM((PLANE, NZ, 128), f32),
            pltpu.VMEM((NZ, PLANE, 128), f32),
            pltpu.VMEM((NZ, PLANE, 128), f32),
            pltpu.VMEM((2, 8, 128), f32),
            pltpu.VMEM((NX, 8, 128), f32),
            dma((2, 4)), dma((2, 4)),
            dma((SLOTS, PLANE - 1)), dma((SLOTS, PLANE - 1)),
            dma((PLANE - 1,)), dma((PLANE - 1,)),
            dma((NZ - 1,)), dma((NZ - 1,)),
            dma((NX - 1,)), dma((NX - 1,)),
        ],
        compiler_params=pltpu.CompilerParams(
            collective_id=0, has_side_effects=True, vmem_limit_bytes=56 * 1024 * 1024
        ),
        cost_estimate=pl.CostEstimate(
            flops=2 * 1536 * 4096 * W, bytes_accessed=8 * 1024 * 1024, transcendentals=2 * 1536 * 4096
        ),
    )(embeddings, pick, bias, pcol)


def solution(mesh):
    return jax.shard_map(
        body,
        mesh=mesh,
        in_specs=(P("blk", None), P(), P()),
        out_specs=P("blk", "rep"),
        check_vma=False,
    )
```

```python
import math

import jax
import jax.numpy as jnp
from jax import lax
from jax.experimental import pallas as pl
from jax.experimental.pallas import tpu as pltpu
from jax.sharding import PartitionSpec as P

W = 1024
BR = 256
BLK_DEV = 6
NY, NZ, NC, NX = 4, 8, 2, 4
PLANE = NY * NC
Q = BR // NX
LANES = NC * Q
NEAR = 3
COLS_A = NEAR * LANES
COLS_F = NX * LANES
LOW = -1e30
TO_BASE2 = math.log2(math.e) / math.sqrt(W)
LN2 = math.log(2.0)
NT = (((1,), (1,)), ((), ()))
MESH = pl.DeviceIdType.MESH
NEAR_DY = (0, 1, NY - 1)
SEEN_AS = (0, 2, 1)


def kernel(
    emb, pick, mask, out,
    q0, ra1, ra2, ra3, rb1, rb2, rb3, r4, g2, emb_v, staged_a, staged_f, held_a, held_f,
    bits, bits_wide, bias_a, bias_f, pcol, row_max, row_sum, far_max, far_sum, far_t, col_max, col_sum,
    col_send_a, col_send_f, col_mid, col_far, col_turn, col_got, row_send, row_got, far_send, far_got,
    in_sem, z_send, z_recv, g_send, g_recv, a_send, a_recv, f_send, f_recv, w_send, w_recv,
    ca_send, ca_recv, cf_send, cf_recv, cz_send, cz_recv, x_send, x_recv, rf_send, rf_recv,
):
    me = lax.axis_index("blk")
    x = lax.axis_index("rep")
    c = lax.rem(me, NC)
    z = lax.rem(me // NC, NZ)
    y = me // (NC * NZ)
    other = 1 - c

    def blk_id(yy, zz, cc):
        return (yy * NZ + zz) * NC + cc

    def zat(dz):
        return lax.rem(z + dz + NZ, NZ)

    def yat(dy):
        return lax.rem(y + dy, NY)

    def xat(dx):
        return lax.rem(x + dx, NX)

    def at(yy, zz, cc, xx):
        return {"blk": blk_id(yy, zz, cc), "rep": xx}

    def core(k):
        return c if k == 0 else other

    far = blk_id(yat(2), z, c)
    far_device = at(yat(2), z, c, x)

    pending = []

    def send(src, dst, ssem, rsem, target):
        copy = pltpu.make_async_remote_copy(
            src_ref=src, dst_ref=dst, send_sem=ssem, recv_sem=rsem, device_id=target, device_id_type=MESH,
        )
        copy.start()
        pending.append(copy)
        return copy

    load_q = pltpu.make_async_copy(emb.at[:, pl.ds(x * Q, Q), :], q0, in_sem.at[0])
    load_e = pltpu.make_async_copy(emb, emb_v, in_sem.at[1])
    load_m = pltpu.make_async_copy(mask.at[me], bits.at[0], in_sem.at[2])
    load_f = pltpu.make_async_copy(mask.at[far], bits.at[1], in_sem.at[3])
    load_q.start()
    load_m.start()
    load_f.start()

    peers = [at(y, zat(dz), c, x) for dz in range(1, NZ)]
    peers += [at(yat(dy), z, core(k), x) for dy in NEAR_DY for k in range(NC) if (dy, k) != (0, 0)]
    peers += [far_device]
    peers += [at(y, z, core(k), xat(dx)) for dx in range(1, NX) for k in range(NC)]
    barrier = pltpu.get_barrier_semaphore()
    for peer in peers:
        pl.semaphore_signal(barrier, inc=1, device_id=peer, device_id_type=MESH)
    load_q.wait()
    load_e.start()
    pl.semaphore_wait(barrier, len(peers))

    ring_a = [q0, ra1, ra2, ra3]
    ring_b = [q0, rb1, rb2, rb3]
    right, left = at(y, zat(1), c, x), at(y, zat(-1), c, x)
    half = BLK_DEV // 2

    def push_ring(d):
        if d < 3:
            return (
                send(ring_a[d], ring_a[d + 1], z_send.at[0, d], z_recv.at[0, d], right),
                send(ring_b[d], ring_b[d + 1], z_send.at[1, d], z_recv.at[1, d], left),
            )
        lo, hi = pl.ds(0, half), pl.ds(half, half)
        return (
            send(ring_a[3].at[lo], r4.at[lo], z_send.at[0, 3], z_recv.at[0, 3], right),
            send(ring_b[3].at[hi], r4.at[hi], z_send.at[1, 3], z_recv.at[1, 3], left),
        )

    near_copies = {}
    far_copies = {}
    passed_on = {}

    def chosen(yy, cc, owner):
        return jnp.clip(pick[blk_id(yy, z, cc), owner], 0, BLK_DEV - 1)

    def stage(slot, ring_ref, zz):
        owner = blk_id(y, zz, c)
        held_f[zz, c] = ring_ref[chosen(yat(2), c, owner)]
        staged_f[slot] = ring_ref[chosen(yat(2), other, owner)]
        mine, theirs = held_f.at[zz, c], staged_f.at[slot]
        routes = [
            (mine, 6 + c, at(y, z, c, xat(1))),
            (mine, 2 + c, at(y, z, c, xat(3))),
            (theirs, 6 + c, at(y, z, other, xat(1))),
            (theirs, 2 + c, at(y, z, other, xat(3))),
            (theirs, c, at(y, z, other, x)),
        ]
        far_copies[slot] = [
            send(src, held_f.at[zz, place], f_send.at[slot, i], f_recv.at[slot, i], target)
            for i, (src, place, target) in enumerate(routes)
        ]
        copies = []
        for n, dy in enumerate(NEAR_DY):
            for k in range(NC):
                rows = ring_ref[chosen(yat(dy), core(k), owner)]
                if (n, k) == (0, 0):
                    held_a[zz, c] = rows
                    continue
                i = n * NC + k - 1
                staged_a[slot, i] = rows
                copies.append(send(
                    staged_a.at[slot, i], held_a.at[zz, SEEN_AS[n] * NC + c],
                    a_send.at[slot, i], a_recv.at[slot, i], at(yat(dy), z, core(k), x),
                ))
        near_copies[slot] = copies

    def forward(slot, zz):
        top, low = pl.ds(0, Q // 2), pl.ds(Q // 2, Q // 2)
        routes = [
            (0, 6 + c, 4 + c, top, xat(1)),
            (1, 2 + c, 4 + c, low, xat(3)),
            (2, 6 + other, 4 + other, top, xat(1)),
            (3, 2 + other, 4 + other, low, xat(3)),
        ]
        copies = []
        for i, place, dest, rows, xx in routes:
            far_copies[slot][i].wait_recv()
            copies.append(send(
                held_f.at[zz, place, rows], held_f.at[zz, dest, rows],
                w_send.at[slot, i], w_recv.at[slot, i], at(y, z, c, xx),
            ))
        passed_on[slot] = copies

    def own_block(a, carry):
        top = pl.multiple_of((x // 2) * LANES, LANES)
        scores = lax.dot_general(
            emb_v[a], emb_v[a, pl.ds(top, LANES), :], NT, preferred_element_type=jnp.float32,
        ) * TO_BASE2
        row = lax.broadcasted_iota(jnp.int32, (BR, LANES), 0)
        col = lax.broadcasted_iota(jnp.int32, (BR, LANES), 1) + top
        valid = (col // Q == x) & (row != col)
        row_max[a] = jnp.where(valid, scores, LOW)
        row_sum[a] = jnp.where(valid, 1.0, 0.0)
        return carry

    def prepare():
        far_max[...] = jnp.full_like(far_max, LOW)
        far_sum[...] = jnp.zeros_like(far_sum)
        row_send[...] = jnp.full_like(row_send, LOW)
        bits_wide[...] = jnp.zeros_like(bits_wide)
        load_m.wait()
        load_f.wait()
        wide = []
        for i in range(2):
            bits_wide[0:64, 0:BLK_DEV] = bits[i].astype(jnp.float32)
            wide.append(bits_wide[...].T[:8])

        def fill(zz, carry):
            p = lax.broadcasted_iota(jnp.int32, (128, COLS_A), 0)
            col = lax.broadcasted_iota(jnp.int32, (128, COLS_A), 1)
            n = col // LANES
            yy = lax.rem(y + jnp.where(n == 2, NY - 1, n), NY)
            owner = blk_id(yy, zz, lax.rem(col // Q, NC))
            live = jnp.dot(wide[0], (p == owner).astype(jnp.float32), preferred_element_type=jnp.float32)
            bias_a[zz] = jnp.where(live > 0.5, 0.0, LOW)
            p = lax.broadcasted_iota(jnp.int32, (128, COLS_F), 0)
            col = lax.broadcasted_iota(jnp.int32, (128, COLS_F), 1)
            owner = blk_id(y, zz, lax.rem(col // Q, NC))
            live = jnp.dot(wide[1], (p == owner).astype(jnp.float32), preferred_element_type=jnp.float32)
            bias_f[zz] = jnp.where(live > 0.5, 0.0, LOW)
            for n, dy in enumerate((0, 1, NY - 1, 2)):
                for cc in range(NC):
                    s = n * NC + cc
                    pcol[zz, s:s + 1, :] = jnp.full((1, 128), pick[blk_id(yat(dy), zz, cc), me], jnp.int32)
            return carry

        lax.fori_loop(0, NZ, fill, 0)
        load_e.wait()
        lax.fori_loop(0, BLK_DEV, own_block, 0)

    def absorb(t, rows, cols, row_at, sum_at):
        parts = [t[:, g * 128:(g + 1) * 128] for g in range(cols // 128)]
        old = row_at[...]
        new = old
        for part in parts:
            new = jnp.maximum(new, part)
        total = sum_at[...] * jnp.exp2(old - new)
        for part in parts:
            total += jnp.exp2(part - new)
        row_at[...] = new
        sum_at[...] = total
        t8 = t.reshape(rows // 8, 8, cols)
        old = col_max[:, :cols]
        new = jnp.maximum(old, jnp.max(t8, axis=0))
        col_sum[:, :cols] = col_sum[:, :cols] * jnp.exp2(old - new) + jnp.sum(jnp.exp2(t8 - new[None]), axis=0)
        col_max[:, :cols] = new

    def clear_cols():
        col_max[...] = jnp.full_like(col_max, LOW)
        col_sum[...] = jnp.zeros_like(col_sum)

    def finish_cols(zz, cols, dest):
        peak = jnp.max(col_max[:, :cols], axis=0, keepdims=True)
        total = jnp.sum(col_sum[:, :cols] * jnp.exp2(col_max[:, :cols] - peak), axis=0, keepdims=True)
        lse = peak + jnp.log2(total)
        for g in range(cols // 128):
            dest[g, pl.ds(zz, 1), :] = lse[:, g * 128:(g + 1) * 128]

    def compute_a(slot, zz):
        for copy in near_copies[slot]:
            copy.wait_recv()
        clear_cols()

        def one(a, carry):
            t = lax.dot_general(
                emb_v[a], held_a[zz].reshape(COLS_A, W), NT, preferred_element_type=jnp.float32,
            ) * TO_BASE2 + bias_a[zz, pl.ds(a, 1), :]
            absorb(t, BR, COLS_A, row_max.at[a], row_sum.at[a])
            return carry

        lax.fori_loop(0, BLK_DEV, one, 0)
        finish_cols(zz, COLS_A, col_send_a)

    def compute_f(slot, zz):
        far_copies[slot][4].wait_recv()
        for copy in passed_on[slot]:
            copy.wait_recv()
        clear_cols()
        far_t[...] = lax.dot_general(
            g2[...].reshape(BLK_DEV * Q, W), held_f[zz].reshape(COLS_F, W), NT,
            preferred_element_type=jnp.float32,
        ).reshape(BLK_DEV, Q, COLS_F)

        def one(a, carry):
            t = far_t[a] * TO_BASE2 + bias_f[zz, pl.ds(a, 1), :]
            absorb(t, Q, COLS_F, far_max.at[a], far_sum.at[a])
            return carry

        lax.fori_loop(0, BLK_DEV, one, 0)
        finish_cols(zz, COLS_F, col_send_f)

    ring = push_ring(0)
    stage(0, q0, z)
    far_rows = send(q0, g2, g_send, g_recv, far_device)
    prepare()
    forward(0, z)
    ready = [(0, z)]
    for d in range(1, 4):
        for copy in ring:
            copy.wait_recv()
        ring = push_ring(d)
        now = [(2 * d - 1, zat(-d)), (2 * d, zat(d))]
        stage(*now[0][:1], ring_a[d], now[0][1])
        stage(*now[1][:1], ring_b[d], now[1][1])
        for item in ready:
            compute_a(*item)
        forward(*now[0])
        if d == 1:
            far_rows.wait_recv()
        for item in ready:
            compute_f(*item)
        forward(*now[1])
        ready = now
    for copy in ring:
        copy.wait_recv()
    last = (7, zat(4))
    stage(7, r4, last[1])
    for item in ready:
        compute_a(*item)
    forward(*last)
    for item in ready:
        compute_f(*item)
    compute_a(*last)

    near_back = []
    for n, dy in enumerate(NEAR_DY):
        for k in range(NC):
            place = SEEN_AS[n] * NC + c
            if (n, k) == (0, 0):
                col_mid[place] = col_send_a[0]
                continue
            i = n * NC + k - 1
            near_back.append(send(
                col_send_a.at[n], col_mid.at[place], ca_send.at[i], ca_recv.at[i], at(yat(dy), z, core(k), x)
            ))
    compute_f(*last)
    far_back = []
    for dx in range(NX):
        for k in range(NC):
            place = (NX - dx) % NX
            if (dx, k) == (0, 0):
                col_far[c, place] = col_send_f[0]
                continue
            i = dx * NC + k - 1
            far_back.append(send(
                col_send_f.at[dx], col_far.at[c, place], cf_send.at[i], cf_recv.at[i], at(y, z, core(k), xat(dx))
            ))

    def row_lse(m, s):
        m, s = m.T, s.T
        peak = jnp.max(m, axis=0, keepdims=True)
        return peak + jnp.log2(jnp.sum(s * jnp.exp2(m - peak), axis=0, keepdims=True))

    for a in range(BLK_DEV):
        lse = row_lse(row_max[a], row_sum[a])
        for h in range(2):
            row_send[h, a:a + 1, :] = lse[:, h * 128:(h + 1) * 128]
    across = []
    for dx in range(1, NX):
        xx = xat(dx)
        across.append(send(
            row_send.at[xx // 2], row_got.at[x], x_send.at[dx - 1], x_recv.at[dx - 1], at(y, z, c, xx)
        ))
    row_got[x] = row_send[x // 2]
    for i in range(BLK_DEV // 2):
        m = far_max[2 * i:2 * i + 2].reshape(LANES, 128)
        s = far_sum[2 * i:2 * i + 2].reshape(LANES, 128)
        far_send[i:i + 1, :] = row_lse(m, s)
    far_back_rows = send(far_send, far_got, rf_send, rf_recv, far_device)

    for copy in [*near_back, *far_back]:
        copy.wait_recv()
    for cc in range(NC):
        v = [col_far[cc, i] for i in range(NX)]
        peak = jnp.maximum(jnp.maximum(v[0], v[1]), jnp.maximum(v[2], v[3]))
        total = sum(jnp.exp2(part - peak) for part in v)
        col_mid[NEAR * NC + cc] = peak + jnp.log2(total)
    for zz in range(NZ):
        for s in range(PLANE):
            col_turn[zz, s:s + 1, :] = col_mid[s, zz:zz + 1, :]
    final = []
    for dz in range(1, NZ):
        zz = zat(dz)
        final.append(send(
            col_turn.at[zz], col_got.at[z], cz_send.at[dz - 1], cz_recv.at[dz - 1], at(y, zz, c, x)
        ))
    col_got[z] = col_turn[z]
    far_back_rows.wait_recv()
    for copy in [*across, *final]:
        copy.wait_recv()

    def to_front(v, shift_it):
        return jnp.where(shift_it, pltpu.roll(v, Q, 1), v)

    got = col_got[...].reshape(NZ * PLANE, 128)
    who = pcol[...].reshape(NZ * PLANE, 128)
    for b in range(BLK_DEV):
        is_it = who == b
        v = jnp.where(is_it, got, LOW)
        peak = jnp.max(v, axis=0, keepdims=True)
        total = jnp.sum(jnp.where(is_it, jnp.exp2(v - peak), 0.0), axis=0, keepdims=True)
        col_max[b:b + 1, 0:128] = peak
        col_sum[b:b + 1, 0:128] = total
        v = far_got[b // 2:b // 2 + 1, :]
        col_max[b:b + 1, 128:256] = v if b % 2 == 0 else pltpu.roll(v, Q, 1)
    col_peak = to_front(col_max[:, 0:128], c == 1)
    col_total = to_front(col_sum[:, 0:128], c == 1)
    rows = [to_front(row_got[i], lax.rem(x, 2) == 1) for i in range(NX)]
    rows.append(col_max[:, 128:256])
    peak = col_peak
    for r in rows:
        peak = jnp.maximum(peak, r)
    total = col_total * jnp.exp2(col_peak - peak)
    for r in rows:
        total += jnp.exp2(r - peak)
    result = (peak + jnp.log2(total)) * LN2
    out[...] = result[:BLK_DEV, :Q]
    for copy in pending:
        copy.wait_send()


def body(embeddings, pick, mask):
    vmem = pl.BlockSpec(memory_space=pltpu.VMEM)
    anywhere = pl.BlockSpec(memory_space=pl.ANY)
    dma = pltpu.SemaphoreType.DMA
    f32, bf16 = jnp.float32, jnp.bfloat16
    slab = pltpu.VMEM((BLK_DEV, Q, W), bf16)
    return pl.pallas_call(
        kernel,
        out_shape=jax.ShapeDtypeStruct((BLK_DEV, Q), f32),
        in_specs=[anywhere, pl.BlockSpec(memory_space=pltpu.SMEM), anywhere],
        out_specs=vmem,
        scratch_shapes=[
            *[slab] * 9,
            pltpu.VMEM((BLK_DEV, BR, W), bf16),
            pltpu.VMEM((NZ, NEAR * NC - 1, Q, W), bf16),
            pltpu.VMEM((NZ, Q, W), bf16),
            pltpu.VMEM((NZ, NEAR * NC, Q, W), bf16),
            pltpu.VMEM((NZ, NX * NC, Q, W), bf16),
            pltpu.VMEM((2, 64, BLK_DEV), jnp.int32),
            pltpu.VMEM((128, 128), f32),
            pltpu.VMEM((NZ, 8, COLS_A), f32),
            pltpu.VMEM((NZ, 8, COLS_F), f32),
            pltpu.VMEM((NZ, PLANE, 128), jnp.int32),
            pltpu.VMEM((BLK_DEV, BR, 128), f32),
            pltpu.VMEM((BLK_DEV, BR, 128), f32),
            pltpu.VMEM((BLK_DEV, Q, 128), f32),
            pltpu.VMEM((BLK_DEV, Q, 128), f32),
            pltpu.VMEM((BLK_DEV, Q, COLS_F), f32),
            pltpu.VMEM((8, COLS_F), f32),
            pltpu.VMEM((8, COLS_F), f32),
            pltpu.VMEM((NEAR, NZ, 128), f32),
            pltpu.VMEM((NX, NZ, 128), f32),
            pltpu.VMEM((PLANE, NZ, 128), f32),
            pltpu.VMEM((NC, NX, NZ, 128), f32),
            pltpu.VMEM((NZ, PLANE, 128), f32),
            pltpu.VMEM((NZ, PLANE, 128), f32),
            pltpu.VMEM((2, 8, 128), f32),
            pltpu.VMEM((NX, 8, 128), f32),
            pltpu.VMEM((8, 128), f32),
            pltpu.VMEM((8, 128), f32),
            dma((4,)),
            dma((2, 4)), dma((2, 4)),
            dma, dma,
            dma((NZ, NEAR * NC - 1)), dma((NZ, NEAR * NC - 1)),
            dma((NZ, 5)), dma((NZ, 5)),
            dma((NZ, 4)), dma((NZ, 4)),
            dma((NEAR * NC - 1,)), dma((NEAR * NC - 1,)),
            dma((PLANE - 1,)), dma((PLANE - 1,)),
            dma((NZ - 1,)), dma((NZ - 1,)),
            dma((NX - 1,)), dma((NX - 1,)),
            dma, dma,
        ],
        compiler_params=pltpu.CompilerParams(
            collective_id=0, has_side_effects=True, vmem_limit_bytes=56 * 1024 * 1024
        ),
        cost_estimate=pl.CostEstimate(
            flops=2 * 1536 * 4096 * W, bytes_accessed=8 * 1024 * 1024, transcendentals=2 * 1536 * 4096
        ),
    )(embeddings.reshape(BLK_DEV, BR, W), pick, mask)


def solution(mesh):
    return jax.shard_map(
        body,
        mesh=mesh,
        in_specs=(P("blk", None), P(), P()),
        out_specs=P("blk", "rep"),
        check_vma=False,
    )
```

```python
import math

import jax
import jax.numpy as jnp
from jax import lax
from jax.experimental import pallas as pl
from jax.experimental.pallas import tpu as pltpu
from jax.sharding import PartitionSpec as P

W = 1024
BR = 256
BLK_DEV = 6
NY, NZ, NC, NX = 4, 8, 2, 4
PLANE = NY * NC
Q = BR // NX
LANES = NC * Q
NEAR = 3
COLS_A = NEAR * LANES
COLS_F = NX * LANES
LOW = -1e30
TO_BASE2 = math.log2(math.e) / math.sqrt(W)
LN2 = math.log(2.0)
NT = (((1,), (1,)), ((), ()))
MESH = pl.DeviceIdType.MESH
NEAR_DY = (0, 1, NY - 1)
SEEN_AS = (0, 2, 1)


def kernel(
    emb, pick_hbm, mask, out,
    pick, q0, a10, a11, a20, a21, a30, a31, b10, b11, b20, b21, b30, b31, r40, r41, g2, emb_v, staged_a, staged_f, held_a, held_f,
    bits, bits_wide, bias_a, bias_f, pcol, row_max, row_sum, far_max, far_sum, t_near, t_far, col_max, col_sum,
    col_send_a, col_send_f, col_mid, col_far, col_turn, col_got, row_send, row_got, far_send, far_got,
    in_sem, z_send, z_recv, g_send, g_recv, a_send, a_recv, f_send, f_recv, w_send, w_recv,
    ca_send, ca_recv, cf_send, cf_recv, cz_send, cz_recv, x_send, x_recv,
):
    me = lax.axis_index("blk")
    x = lax.axis_index("rep")
    c = lax.rem(me, NC)
    z = lax.rem(me // NC, NZ)
    y = me // (NC * NZ)
    other = 1 - c

    def blk_id(yy, zz, cc):
        return (yy * NZ + zz) * NC + cc

    def zat(dz):
        return lax.rem(z + dz + NZ, NZ)

    def yat(dy):
        return lax.rem(y + dy, NY)

    def xat(dx):
        return lax.rem(x + dx, NX)

    def at(yy, zz, cc, xx):
        return {"blk": blk_id(yy, zz, cc), "rep": xx}

    def core(k):
        return c if k == 0 else other

    far = blk_id(yat(2), z, c)
    far_device = at(yat(2), z, c, x)

    def send(src, dst, ssem, rsem, target):
        pltpu.make_async_remote_copy(
            src_ref=src, dst_ref=dst, send_sem=ssem, recv_sem=rsem, device_id=target, device_id_type=MESH,
        ).start()

    def await_bytes(like, sem):
        pltpu.make_async_copy(like, like, sem).wait()

    load_q = pltpu.make_async_copy(emb.at[:, pl.ds(x * Q, Q), :], q0, in_sem.at[0])
    load_e = pltpu.make_async_copy(emb, emb_v, in_sem.at[1])
    load_p = pltpu.make_async_copy(pick_hbm, pick, in_sem.at[3])
    load_m = pltpu.make_async_copy(mask, bits, in_sem.at[2])
    load_q.start()
    load_p.start()
    load_m.start()

    peers = [at(y, zat(dz), c, x) for dz in (1, -1)]
    peers += [at(yat(dy), z, core(k), x) for dy in NEAR_DY for k in range(NC) if (dy, k) != (0, 0)]
    peers += [far_device]
    peers += [at(y, z, core(k), xat(dx)) for dx in (1, NX - 1) for k in range(NC)]
    barrier = pltpu.get_barrier_semaphore()
    for peer in peers:
        pl.semaphore_signal(barrier, inc=1, device_id=peer, device_id_type=MESH)
    load_q.wait()
    load_p.wait()
    load_e.start()
    pl.semaphore_wait(barrier, len(peers))

    part = [pl.ds(0, Q // 2), pl.ds(Q // 2, Q // 2)]
    own = (q0.at[:, part[0]], q0.at[:, part[1]])
    r4 = (r40, r41)
    ring_a = [own, (a10, a11), (a20, a21), (a30, a31)]
    ring_b = [own, (b10, b11), (b20, b21), (b30, b31)]
    right, left = at(y, zat(1), c, x), at(y, zat(-1), c, x)
    def push_ring(d, h):
        for i, (chain, target) in enumerate(((ring_a, right), (ring_b, left))):
            if d < 3 or i == h:
                dst = chain[d + 1] if d < 3 else r4
                send(chain[d][h], dst[h], z_send, z_recv.at[d, h if d < 3 else 0], target)

    def await_ring(d, h):
        if d < 3:
            await_bytes(q0, z_recv.at[d, h])
        else:
            await_bytes(q0, z_recv.at[3, 0])

    def chosen(yy, cc, owner):
        return jnp.clip(pick[blk_id(yy, z, cc), owner], 0, BLK_DEV - 1)

    def stage_far(slot, ring_ref, zz, h):
        owner = blk_id(y, zz, c)
        held_f[slot, c, part[h]] = ring_ref[h][chosen(yat(2), c, owner)]
        staged_f[slot, part[h]] = ring_ref[h][chosen(yat(2), other, owner)]
        mine, theirs = held_f.at[slot, c, part[h]], staged_f.at[slot, part[h]]
        routes = [
            (mine, 6 + c, at(y, z, c, xat(1))),
            (mine, 2 + c, at(y, z, c, xat(3))),
            (theirs, 6 + c, at(y, z, other, xat(1))),
            (theirs, 2 + c, at(y, z, other, xat(3))),
            (theirs, c, at(y, z, other, x)),
        ]
        for i, (src, place, target) in enumerate(routes):
            goes_on = i < 4 and i % 2 == h
            send(
                src, held_f.at[slot, place, part[h]], f_send, f_recv.at[slot, h] if goes_on else w_recv.at[slot], target
            )

    def stage_near(slot, ring_ref, zz):
        owner = blk_id(y, zz, c)
        for n, dy in enumerate(NEAR_DY):
            for k in range(NC):
                index = chosen(yat(dy), core(k), owner)
                i = n * NC + k - 1
                for h in range(2):
                    if i < 0:
                        held_a[slot, c, part[h]] = ring_ref[h][index]
                    else:
                        staged_a[slot, i, part[h]] = ring_ref[h][index]
                if i < 0:
                    continue
                send(
                    staged_a.at[slot, i], held_a.at[slot, SEEN_AS[n] * NC + c],
                    a_send, a_recv.at[slot], at(yat(dy), z, core(k), x),
                )

    def forward(slot, zz, h):
        await_bytes(staged_f.at[slot], f_recv.at[slot, h])
        for k in range(NC):
            place = (6, 2)[h] + core(k)
            send(
                held_f.at[slot, place, part[h]], held_f.at[slot, 4 + core(k), part[h]],
                w_send, w_recv.at[slot], at(y, z, c, xat((1, 3)[h])),
            )

    def own_block(a, carry):
        top = pl.multiple_of((x // 2) * LANES, LANES)
        scores = lax.dot_general(
            emb_v[a], emb_v[a, pl.ds(top, LANES), :], NT, preferred_element_type=jnp.float32,
        ) * TO_BASE2
        row = lax.broadcasted_iota(jnp.int32, (BR, LANES), 0)
        col = lax.broadcasted_iota(jnp.int32, (BR, LANES), 1) + top
        valid = (col // Q == x) & (row != col)
        row_max[a] = jnp.where(valid, scores, LOW)
        row_sum[a] = jnp.where(valid, 1.0, 0.0)
        return carry

    def prepare():
        far_max[...] = jnp.full_like(far_max, LOW)
        far_sum[...] = jnp.zeros_like(far_sum)
        row_send[...] = jnp.full_like(row_send, LOW)
        bits_wide[...] = jnp.zeros_like(bits_wide)
        load_m.wait()
        for i, row in enumerate((me, far)):
            for a in range(BLK_DEV):
                bits_wide[i, a:a + 1, 0:64] = bits[a, pl.ds(row, 1), :].astype(jnp.float32)
        wide = [bits_wide[i] for i in range(2)]

        def fill(slot, carry):
            d = (slot + 1) // 2
            zz = lax.rem(z + d - 2 * d * lax.rem(slot, 2) + NZ, NZ)
            p = lax.broadcasted_iota(jnp.int32, (128, COLS_A), 0)
            col = lax.broadcasted_iota(jnp.int32, (128, COLS_A), 1)
            n = col // LANES
            yy = lax.rem(y + jnp.where(n == 2, NY - 1, n), NY)
            owner = blk_id(yy, zz, lax.rem(col // Q, NC))
            live = jnp.dot(wide[0], (p == owner).astype(jnp.float32), preferred_element_type=jnp.float32)
            bias_a[slot] = jnp.where(live > 0.5, 0.0, LOW)
            p = lax.broadcasted_iota(jnp.int32, (128, COLS_F), 0)
            col = lax.broadcasted_iota(jnp.int32, (128, COLS_F), 1)
            owner = blk_id(y, zz, lax.rem(col // Q, NC))
            live = jnp.dot(wide[1], (p == owner).astype(jnp.float32), preferred_element_type=jnp.float32)
            bias_f[slot] = jnp.where(live > 0.5, 0.0, LOW)
            for n, dy in enumerate((0, 1, NY - 1, 2)):
                for cc in range(NC):
                    s = n * NC + cc
                    pcol[zz, s:s + 1, :] = jnp.full((1, 128), pick[blk_id(yat(dy), zz, cc), me], jnp.int32)
            return carry

        lax.fori_loop(0, NZ, fill, 0)
        load_e.wait()
        lax.fori_loop(0, BLK_DEV, own_block, 0)

    def absorb(t, cols, row_at, sum_at):
        parts = [t[:, g * 128:(g + 1) * 128] for g in range(cols // 128)]
        old = row_at[...]
        new = old
        for p in parts:
            new = jnp.maximum(new, p)
        total = sum_at[...] * jnp.exp2(old - new)
        for p in parts:
            total += jnp.exp2(p - new)
        row_at[...] = new
        sum_at[...] = total
        t8 = t.reshape(t.shape[0] // 8, 8, cols)
        old = col_max[:, :cols]
        new = jnp.maximum(old, jnp.max(t8, axis=0))
        col_sum[:, :cols] = col_sum[:, :cols] * jnp.exp2(old - new) + jnp.sum(jnp.exp2(t8 - new[None]), axis=0)
        col_max[:, :cols] = new

    def score(items, blocks, held, bias, width, t_ref, row_at, sum_at, dest):
        first, count = items[0][0], len(items)
        cols = count * width
        col_max[...] = jnp.full_like(col_max, LOW)
        col_sum[...] = jnp.zeros_like(col_sum)

        def product(g):
            lhs = blocks[g]
            t_ref[g % 2, :lhs.shape[0], :cols] = lax.dot_general(
                lhs, held[first:first + count].reshape(cols, W), NT, preferred_element_type=jnp.float32,
            )

        def sums(g):
            per = BLK_DEV // len(blocks)
            rows = blocks[g].shape[0] // per
            for i in range(per):
                a = g * per + i
                shift = jnp.concatenate([bias[slot, a:a + 1, :] for slot, _ in items], axis=1)
                absorb(
                    t_ref[g % 2, i * rows:(i + 1) * rows, :cols] * TO_BASE2 + shift, cols, row_at.at[a], sum_at.at[a]
                )

        product(0)
        for g in range(1, len(blocks)):
            product(g)
            sums(g - 1)
        sums(len(blocks) - 1)
        peak = jnp.max(col_max[:, :cols], axis=0, keepdims=True)
        total = jnp.sum(col_sum[:, :cols] * jnp.exp2(col_max[:, :cols] - peak), axis=0, keepdims=True)
        lse = peak + jnp.log2(total)
        for n, (_, zz) in enumerate(items):
            for g in range(width // 128):
                lo = n * width + g * 128
                dest[g, pl.ds(zz, 1), :] = lse[:, lo:lo + 128]

    def compute_a(items):
        for slot, _ in items:
            await_bytes(staged_a.at[slot], a_recv.at[slot])
        blocks = [emb_v[a] for a in range(BLK_DEV)]
        score(items, blocks, held_a, bias_a, COLS_A, t_near, row_max, row_sum, col_send_a)

    def compute_f(items):
        for slot, _ in items:
            await_bytes(staged_a.at[slot], w_recv.at[slot])
        blocks = [g2[2 * g:2 * g + 2].reshape(2 * Q, W) for g in range(BLK_DEV // 2)]
        score(items, blocks, held_f, bias_f, COLS_F, t_far, far_max, far_sum, col_send_f)

    push_ring(0, 0)
    push_ring(0, 1)
    stage_far(0, own, z, 0)
    stage_far(0, own, z, 1)
    send(q0, g2, g_send, g_recv, far_device)
    stage_near(0, own, z)
    prepare()
    forward(0, z, 0)
    ready, late = [(0, z)], []
    for d in range(1, 4):
        now = [(2 * d - 1, ring_a[d], zat(-d)), (2 * d, ring_b[d], zat(d))]
        for h in range(2):
            await_ring(d - 1, h)
            push_ring(d, h)
            for item in now:
                stage_far(*item, h)
            if h == 0:
                for item in ready:
                    forward(*item, 1)
                if d == 2:
                    await_bytes(q0, g_recv)
                if late:
                    compute_f(late)
            else:
                for item in now:
                    stage_near(*item)
                now = [(slot, zz) for slot, _, zz in now]
                for item in now:
                    forward(*item, 0)
                compute_a(ready)
        ready, late = now, ready
    last = (7, zat(4))
    await_ring(3, 0)
    for h in range(2):
        stage_far(7, r4, last[1], h)
    stage_near(7, r4, last[1])
    for item in ready:
        forward(*item, 1)
    compute_f(late)
    compute_a(ready)
    forward(*last, 0)
    forward(*last, 1)
    compute_f(ready)
    compute_a([last])

    for n, dy in enumerate(NEAR_DY):
        for k in range(NC):
            place = SEEN_AS[n] * NC + c
            if (n, k) == (0, 0):
                col_mid[place] = col_send_a[0]
                continue
            send(col_send_a.at[n], col_mid.at[place], ca_send, ca_recv, at(yat(dy), z, core(k), x))
    compute_f([last])
    for dx in range(NX):
        for k in range(NC):
            place = (NX - dx) % NX
            if (dx, k) == (0, 0):
                col_far[c, place] = col_send_f[0]
                continue
            send(col_send_f.at[dx], col_far.at[c, place], cf_send, cf_recv, at(y, z, core(k), xat(dx)))

    def row_lse(m, s):
        v = (m + jnp.log2(jnp.maximum(s, 1.0))).T
        peak = jnp.max(v, axis=0, keepdims=True)
        return peak + jnp.log2(jnp.sum(jnp.exp2(v - peak), axis=0, keepdims=True))

    for a in range(BLK_DEV):
        lse = row_lse(row_max[a], row_sum[a])
        for h in range(2):
            row_send[h, a:a + 1, :] = lse[:, h * 128:(h + 1) * 128]
    for dx in range(1, NX):
        xx = xat(dx)
        send(row_send.at[xx // 2], row_got.at[x], x_send, x_recv, at(y, z, c, xx))
    row_got[x] = row_send[x // 2]
    for i in range(BLK_DEV // 2):
        m = far_max[2 * i:2 * i + 2].reshape(LANES, 128)
        s = far_sum[2 * i:2 * i + 2].reshape(LANES, 128)
        far_send[i:i + 1, :] = row_lse(m, s)
    send(far_send, far_got, x_send, x_recv, far_device)

    await_bytes(col_got.at[pl.ds(0, 5)], ca_recv)
    await_bytes(col_got.at[pl.ds(0, 7)], cf_recv)
    for cc in range(NC):
        v = [col_far[cc, i] for i in range(NX)]
        peak = jnp.maximum(jnp.maximum(v[0], v[1]), jnp.maximum(v[2], v[3]))
        total = sum(jnp.exp2(part - peak) for part in v)
        col_mid[NEAR * NC + cc] = peak + jnp.log2(total)
    for zz in range(NZ):
        for s in range(PLANE):
            col_turn[zz, s:s + 1, :] = col_mid[s, zz:zz + 1, :]
    for dz in range(1, NZ):
        zz = zat(dz)
        send(col_turn.at[zz], col_got.at[z], cz_send, cz_recv, at(y, zz, c, x))
    col_got[z] = col_turn[z]
    await_bytes(row_got, x_recv)
    await_bytes(col_turn.at[pl.ds(0, 7)], cz_recv)

    def to_front(v, shift_it):
        return jnp.where(shift_it, pltpu.roll(v, Q, 1), v)

    got = col_got[...].reshape(NZ * PLANE, 128)
    who = pcol[...].reshape(NZ * PLANE, 128)
    for b in range(BLK_DEV):
        is_it = who == b
        v = jnp.where(is_it, got, LOW)
        peak = jnp.max(v, axis=0, keepdims=True)
        total = jnp.sum(jnp.where(is_it, jnp.exp2(v - peak), 0.0), axis=0, keepdims=True)
        col_max[b:b + 1, 0:128] = peak
        col_sum[b:b + 1, 0:128] = total
        v = far_got[b // 2:b // 2 + 1, :]
        col_max[b:b + 1, 128:256] = v if b % 2 == 0 else pltpu.roll(v, Q, 1)
    col_peak = to_front(col_max[:, 0:128], c == 1)
    col_total = to_front(col_sum[:, 0:128], c == 1)
    rows = [to_front(row_got[i], lax.rem(x, 2) == 1) for i in range(NX)]
    rows.append(col_max[:, 128:256])
    peak = col_peak
    for r in rows:
        peak = jnp.maximum(peak, r)
    total = col_total * jnp.exp2(col_peak - peak)
    for r in rows:
        total += jnp.exp2(r - peak)
    result = peak + jnp.log2(total)
    out[...] = result[:BLK_DEV, :Q]
    await_bytes(held_a.at[pl.ds(0, 7)], z_send)
    await_bytes(q0, g_send)
    await_bytes(staged_a, a_send)
    await_bytes(staged_a, f_send)
    await_bytes(held_f.at[pl.ds(0, 2)], w_send)
    await_bytes(col_turn.at[pl.ds(0, 5)], ca_send)
    await_bytes(col_turn.at[pl.ds(0, 7)], cf_send)
    await_bytes(col_turn.at[pl.ds(0, 7)], cz_send)
    await_bytes(row_got, x_send)


def body(embeddings, pick, mask):
    vmem = pl.BlockSpec(memory_space=pltpu.VMEM)
    anywhere = pl.BlockSpec(memory_space=pl.ANY)
    dma = pltpu.SemaphoreType.DMA
    f32, bf16 = jnp.float32, jnp.bfloat16
    slab = pltpu.VMEM((BLK_DEV, Q, W), bf16)
    base2 = pl.pallas_call(
        kernel,
        out_shape=jax.ShapeDtypeStruct((BLK_DEV, Q), f32),
        in_specs=[anywhere, anywhere, anywhere],
        out_specs=vmem,
        scratch_shapes=[
            pltpu.SMEM((64, 64), jnp.int32),
            slab,
            *[pltpu.VMEM((BLK_DEV, Q // 2, W), bf16)] * 14,
            slab,
            pltpu.VMEM((BLK_DEV, BR, W), bf16),
            pltpu.VMEM((NZ, NEAR * NC - 1, Q, W), bf16),
            pltpu.VMEM((NZ, Q, W), bf16),
            pltpu.VMEM((NZ, NEAR * NC, Q, W), bf16),
            pltpu.VMEM((NZ, NX * NC, Q, W), bf16),
            pltpu.VMEM((BLK_DEV, 64, 64), jnp.int32),
            pltpu.VMEM((2, 8, 128), f32),
            pltpu.VMEM((NZ, 8, COLS_A), f32),
            pltpu.VMEM((NZ, 8, COLS_F), f32),
            pltpu.VMEM((NZ, PLANE, 128), jnp.int32),
            pltpu.VMEM((BLK_DEV, BR, 128), f32),
            pltpu.VMEM((BLK_DEV, BR, 128), f32),
            pltpu.VMEM((BLK_DEV, Q, 128), f32),
            pltpu.VMEM((BLK_DEV, Q, 128), f32),
            pltpu.VMEM((2, BR, 2 * COLS_A), f32),
            pltpu.VMEM((2, 2 * Q, 2 * COLS_F), f32),
            pltpu.VMEM((8, 2 * COLS_F), f32),
            pltpu.VMEM((8, 2 * COLS_F), f32),
            pltpu.VMEM((NEAR, NZ, 128), f32),
            pltpu.VMEM((NX, NZ, 128), f32),
            pltpu.VMEM((PLANE, NZ, 128), f32),
            pltpu.VMEM((NC, NX, NZ, 128), f32),
            pltpu.VMEM((NZ, PLANE, 128), f32),
            pltpu.VMEM((NZ, PLANE, 128), f32),
            pltpu.VMEM((2, 8, 128), f32),
            pltpu.VMEM((NX, 8, 128), f32),
            pltpu.VMEM((8, 128), f32),
            pltpu.VMEM((8, 128), f32),
            dma((4,)),
            dma, dma((4, 2)),
            dma, dma,
            dma, dma((NZ,)),
            dma, dma((NZ, 2)),
            dma, dma((NZ,)),
            *[dma] * 8,
        ],
        compiler_params=pltpu.CompilerParams(
            collective_id=0, has_side_effects=True, vmem_limit_bytes=56 * 1024 * 1024
        ),
        cost_estimate=pl.CostEstimate(
            flops=2 * 1536 * 4096 * W, bytes_accessed=8 * 1024 * 1024, transcendentals=2 * 1536 * 4096
        ),
    )(embeddings.reshape(BLK_DEV, BR, W), pick, mask.transpose(2, 0, 1))
    return base2 * LN2


def solution(mesh):
    return jax.shard_map(
        body,
        mesh=mesh,
        in_specs=(P("blk", None), P(), P()),
        out_specs=P("blk", "rep"),
        check_vma=False,
    )
```

```python
import math

import jax
import jax.numpy as jnp
from jax import lax
from jax.experimental import pallas as pl
from jax.experimental.pallas import tpu as pltpu
from jax.sharding import PartitionSpec as P

W = 1024
BR = 256
BLK_DEV = 6
NY, NZ, NC, NX = 4, 8, 2, 4
PLANE = NY * NC
Q = BR // NX
LANES = NC * Q
NEAR = 3
COLS_A = NEAR * LANES
COLS_F = NX * LANES
LOW = -1e30
TO_BASE2 = math.log2(math.e) / math.sqrt(W)
LN2 = math.log(2.0)
NT = (((1,), (1,)), ((), ()))
MESH = pl.DeviceIdType.MESH
NEAR_DY = (0, 1, NY - 1)
SEEN_AS = (0, 2, 1)


def kernel(
    emb, pick_hbm, mask, out,
    pick, q0, a10, a11, a20, a21, a30, a31, b10, b11, b20, b21, b30, b31, r400, r401, r410, r411, g2, emb_v, staged_a, staged_f, held_a, held_f,
    bits, bits_wide, bias_a, bias_f, pcol, row_max, row_sum, far_max, far_sum, t_near, t_far, col_max, col_sum,
    col_send_a, col_send_f, col_mid, col_far, col_turn, col_got, row_send, row_got, far_send, far_got,
    last_a, last_f, end_near, end_far,
    in_sem, z_send, z_recv, g_send, g_recv, a_send, a_recv, f_send, f_recv, w_send, w_recv,
    ca_send, ca_recv, cf_send, cf_recv, cz_send, cz_recv, x_send, x_recv,
    ea_send, ea_recv, ef_send, ef_recv,
):
    me = lax.axis_index("blk")
    x = lax.axis_index("rep")
    c = lax.rem(me, NC)
    z = lax.rem(me // NC, NZ)
    y = me // (NC * NZ)
    other = 1 - c

    def blk_id(yy, zz, cc):
        return (yy * NZ + zz) * NC + cc

    def zat(dz):
        return lax.rem(z + dz + NZ, NZ)

    def yat(dy):
        return lax.rem(y + dy, NY)

    def xat(dx):
        return lax.rem(x + dx, NX)

    def at(yy, zz, cc, xx):
        return {"blk": blk_id(yy, zz, cc), "rep": xx}

    def core(k):
        return c if k == 0 else other

    far = blk_id(yat(2), z, c)
    far_device = at(yat(2), z, c, x)

    def send(src, dst, ssem, rsem, target):
        pltpu.make_async_remote_copy(
            src_ref=src, dst_ref=dst, send_sem=ssem, recv_sem=rsem, device_id=target, device_id_type=MESH,
        ).start()

    def await_bytes(like, sem):
        pltpu.make_async_copy(like, like, sem).wait()

    load_q = pltpu.make_async_copy(emb.at[:, pl.ds(x * Q, Q), :], q0, in_sem.at[0])
    load_e = pltpu.make_async_copy(emb, emb_v, in_sem.at[1])
    load_p = pltpu.make_async_copy(pick_hbm, pick, in_sem.at[3])
    load_m = pltpu.make_async_copy(mask, bits, in_sem.at[2])
    load_q.start()
    load_p.start()
    load_m.start()

    peers = [at(y, zat(dz), c, x) for dz in (1, -1)]
    peers += [at(yat(dy), z, core(k), x) for dy in NEAR_DY for k in range(NC) if (dy, k) != (0, 0)]
    peers += [far_device]
    peers += [at(y, z, core(k), xat(dx)) for dx in (1, NX - 1) for k in range(NC)]
    barrier = pltpu.get_barrier_semaphore()
    for peer in peers:
        pl.semaphore_signal(barrier, inc=1, device_id=peer, device_id_type=MESH)
    load_q.wait()
    load_p.wait()
    load_e.start()
    pl.semaphore_wait(barrier, len(peers))

    part = [pl.ds(0, Q // 2), pl.ds(Q // 2, Q // 2)]
    own = (q0.at[:, part[0]], q0.at[:, part[1]])
    r4 = ((r400, r401), (r410, r411))
    ring_a = [own, (a10, a11), (a20, a21), (a30, a31)]
    ring_b = [own, (b10, b11), (b20, b21), (b30, b31)]
    right, left = at(y, zat(1), c, x), at(y, zat(-1), c, x)
    def push_ring(d, turn):
        for i, (chain, target) in enumerate(((ring_a, right), (ring_b, left))):
            h = (turn + i) % 2
            if d < 3:
                send(chain[d][h], chain[d + 1][h], z_send, z_recv.at[d, turn], target)
            elif turn == 0:
                for r in range(2):
                    send(chain[d][h].at[:, pl.ds(r * Q // 4, Q // 4)], r4[h][r], z_send, z_recv.at[d, r], target)

    def await_ring(d, turn):
        await_bytes(q0 if d < 3 else a10, z_recv.at[d, turn])

    def chosen(yy, cc, owner):
        return jnp.clip(pick[blk_id(yy, z, cc), owner], 0, BLK_DEV - 1)

    def stage_far(slot, slab, zz, h, lo, count, first):
        owner = blk_id(y, zz, c)
        rows = pl.ds(lo, count)
        held_f[slot, c, rows] = slab[chosen(yat(2), c, owner)]
        staged_f[slot, rows] = slab[chosen(yat(2), other, owner)]
        mine, theirs = held_f.at[slot, c, rows], staged_f.at[slot, rows]
        routes = [
            (mine, 6 + c, at(y, z, c, xat(1))),
            (mine, 2 + c, at(y, z, c, xat(3))),
            (theirs, 6 + c, at(y, z, other, xat(1))),
            (theirs, 2 + c, at(y, z, other, xat(3))),
            (theirs, c, at(y, z, other, x)),
        ]
        order = (0, 2, 1, 3, 4) if h == 0 else (1, 3, 0, 2, 4)
        for i in order:
            src, place, target = routes[i]
            goes_on = i < 4 and i % 2 == h
            send(
                src, held_f.at[slot, place, rows], f_send, f_recv.at[first, h] if goes_on else w_recv.at[slot], target
            )

    def stage_near(slot, slabs, zz):
        owner = blk_id(y, zz, c)
        for n, dy in enumerate(NEAR_DY):
            for k in range(NC):
                index = chosen(yat(dy), core(k), owner)
                i = n * NC + k - 1
                count = Q // len(slabs)
                for g, slab in enumerate(slabs):
                    rows = pl.ds(g * count, count)
                    if i < 0:
                        held_a[slot, c, rows] = slab[index]
                    else:
                        staged_a[slot, i, rows] = slab[index]
                if i < 0:
                    continue
                send(
                    staged_a.at[slot, i], held_a.at[slot, SEEN_AS[n] * NC + c],
                    a_send, a_recv.at[slot], at(yat(dy), z, core(k), x),
                )

    def forward(slot, h, lo, count, first):
        rows = pl.ds(lo, count)
        await_bytes(staged_f.at[0, pl.ds(0, 2 * count)], f_recv.at[first, h])
        for k in range(NC):
            place = (6, 2)[h] + core(k)
            send(
                held_f.at[slot, place, rows], held_f.at[slot, 4 + core(k), rows],
                w_send, w_recv.at[slot], at(y, z, c, xat((1, 3)[h])),
            )

    def own_block(a, carry):
        top = pl.multiple_of((x // 2) * LANES, LANES)
        scores = lax.dot_general(
            emb_v[a], emb_v[a, pl.ds(top, LANES), :], NT, preferred_element_type=jnp.float32,
        ) * TO_BASE2
        row = lax.broadcasted_iota(jnp.int32, (BR, LANES), 0)
        col = lax.broadcasted_iota(jnp.int32, (BR, LANES), 1) + top
        valid = (col // Q == x) & (row != col)
        row_max[a] = jnp.where(valid, scores, LOW)
        row_sum[a] = jnp.where(valid, 1.0, 0.0)
        return carry

    def prepare():
        far_max[...] = jnp.full_like(far_max, LOW)
        far_sum[...] = jnp.zeros_like(far_sum)
        for ref in (row_send, far_send, col_send_a, col_send_f):
            ref[...] = jnp.full_like(ref, LOW)
        bits_wide[...] = jnp.zeros_like(bits_wide)
        load_m.wait()
        for i, row in enumerate((me, far)):
            for a in range(BLK_DEV):
                bits_wide[i, a:a + 1, 0:64] = bits[a, pl.ds(row, 1), :].astype(jnp.float32)
        wide = [bits_wide[i] for i in range(2)]

        def fill(slot, carry):
            d = (slot + 1) // 2
            zz = lax.rem(z + d - 2 * d * lax.rem(slot, 2) + NZ, NZ)
            p = lax.broadcasted_iota(jnp.int32, (128, COLS_A), 0)
            col = lax.broadcasted_iota(jnp.int32, (128, COLS_A), 1)
            n = col // LANES
            yy = lax.rem(y + jnp.where(n == 2, NY - 1, n), NY)
            owner = blk_id(yy, zz, lax.rem(col // Q, NC))
            live = jnp.dot(wide[0], (p == owner).astype(jnp.float32), preferred_element_type=jnp.float32)
            bias_a[slot] = jnp.where(live > 0.5, 0.0, LOW)
            p = lax.broadcasted_iota(jnp.int32, (128, COLS_F), 0)
            col = lax.broadcasted_iota(jnp.int32, (128, COLS_F), 1)
            owner = blk_id(y, zz, lax.rem(col // Q, NC))
            live = jnp.dot(wide[1], (p == owner).astype(jnp.float32), preferred_element_type=jnp.float32)
            bias_f[slot] = jnp.where(live > 0.5, 0.0, LOW)
            for n, dy in enumerate((0, 1, NY - 1, 2)):
                for cc in range(NC):
                    s = n * NC + cc
                    pcol[zz, s:s + 1, :] = jnp.full((1, 128), pick[blk_id(yat(dy), zz, cc), me], jnp.int32)
            return carry

        lax.fori_loop(0, NZ, fill, 0)
        load_e.wait()
        lax.fori_loop(0, BLK_DEV, own_block, 0)

    def absorb(t, cols, row_at, sum_at):
        parts = [t[:, g * 128:(g + 1) * 128] for g in range(cols // 128)]
        old = row_at[...]
        new = old
        for p in parts:
            new = jnp.maximum(new, p)
        total = sum_at[...] * jnp.exp2(old - new)
        for p in parts:
            total += jnp.exp2(p - new)
        row_at[...] = new
        sum_at[...] = total
        t8 = t.reshape(t.shape[0] // 8, 8, cols)
        old = col_max[:, :cols]
        new = jnp.maximum(old, jnp.max(t8, axis=0))
        col_sum[:, :cols] = col_sum[:, :cols] * jnp.exp2(old - new) + jnp.sum(jnp.exp2(t8 - new[None]), axis=0)
        col_max[:, :cols] = new

    def score(items, blocks, held, bias, width, t_ref, row_at, sum_at, dest, alone):
        first, count = items[0][0], len(items)
        cols = count * width
        col_max[...] = jnp.full_like(col_max, LOW)
        col_sum[...] = jnp.zeros_like(col_sum)

        def product(g):
            lhs = blocks[g]
            t_ref[g % 2, :lhs.shape[0], :cols] = lax.dot_general(
                lhs, held[first:first + count].reshape(cols, W), NT, preferred_element_type=jnp.float32,
            )

        def sums(g):
            per = BLK_DEV // len(blocks)
            rows = blocks[g].shape[0] // per
            for i in range(per):
                a = g * per + i
                shift = jnp.concatenate([bias[slot, a:a + 1, :] for slot, _ in items], axis=1)
                absorb(
                    t_ref[g % 2, i * rows:(i + 1) * rows, :cols] * TO_BASE2 + shift, cols, row_at.at[a], sum_at.at[a]
                )

        product(0)
        for g in range(1, len(blocks)):
            product(g)
            sums(g - 1)
        sums(len(blocks) - 1)
        peak = jnp.max(col_max[:, :cols], axis=0, keepdims=True)
        total = jnp.sum(col_sum[:, :cols] * jnp.exp2(col_max[:, :cols] - peak), axis=0, keepdims=True)
        lse = peak + jnp.log2(total)
        for n, (_, zz) in enumerate(items):
            for g in range(width // 128):
                lo = n * width + g * 128
                if not alone:
                    dest[g, pl.ds(zz, 1), :] = lse[:, lo:lo + 128]
                else:
                    dest[g] = jnp.broadcast_to(lse[:, lo:lo + 128], (8, 128))

    def compute_a(items, dest=col_send_a, alone=False):
        for slot, _ in items:
            await_bytes(staged_a.at[slot], a_recv.at[slot])
        blocks = [emb_v[a] for a in range(BLK_DEV)]
        score(items, blocks, held_a, bias_a, COLS_A, t_near, row_max, row_sum, dest, alone)

    def compute_f(items, dest=col_send_f, alone=False):
        for slot, _ in items:
            await_bytes(staged_a.at[slot], w_recv.at[slot])
        blocks = [g2[2 * g:2 * g + 2].reshape(2 * Q, W) for g in range(BLK_DEV // 2)]
        score(items, blocks, held_f, bias_f, COLS_F, t_far, far_max, far_sum, dest, alone)

    push_ring(0, 0)
    push_ring(0, 1)
    for h in range(2):
        stage_far(0, own[h], z, h, h * Q // 2, Q // 2, 0)
    send(q0, g2, g_send, g_recv, far_device)
    stage_near(0, own, z)
    prepare()
    forward(0, 0, 0, Q // 2, 0)
    ready, late = [(0, z)], []
    for d in range(1, 4):
        now = [(2 * d - 1, zat(-d)), (2 * d, zat(d))]
        chains = [ring_a[d], ring_b[d]]
        for turn in range(2):
            await_ring(d - 1, turn)
            push_ring(d, turn)
            for i, (slot, zz) in enumerate(now):
                h = (turn + i) % 2
                stage_far(slot, chains[i][h], zz, h, h * Q // 2, Q // 2, slot)
            if turn == 0:
                if d == 1:
                    forward(0, 1, Q // 2, Q // 2, 0)
                    continue
                for i, (slot, _) in enumerate(ready):
                    h = (1 + i) % 2
                    forward(slot, h, h * Q // 2, Q // 2, slot)
                if d == 2:
                    await_bytes(q0, g_recv)
                compute_f(late)
            else:
                for i, (slot, zz) in enumerate(now):
                    stage_near(slot, chains[i], zz)
                for i, (slot, _) in enumerate(now):
                    forward(slot, i, i * Q // 2, Q // 2, slot)
                compute_a(ready)
        ready, late = now, ready
    for i, (slot, _) in enumerate(ready):
        h = (1 + i) % 2
        forward(slot, h, h * Q // 2, Q // 2, slot)
    compute_f(late)
    last = (7, zat(4))
    rounds = [(h, h * Q // 2 + r * Q // 4, Q // 4, 7 + r) for r in range(2) for h in range(2)]
    for r in range(2):
        await_ring(3, r)
        for h, lo, count, first in rounds[2 * r:2 * r + 2]:
            stage_far(7, r4[h][r], last[1], h, lo, count, first)
    stage_near(7, (*r4[0], *r4[1]), last[1])
    compute_a(ready)
    for h, lo, count, first in rounds[:2]:
        forward(7, h, lo, count, first)
    compute_f(ready)
    for h, lo, count, first in rounds[2:]:
        forward(7, h, lo, count, first)

    for n, dy in enumerate(NEAR_DY):
        for k in range(NC):
            place = SEEN_AS[n] * NC + c
            if (n, k) == (0, 0):
                col_mid[place] = col_send_a[0]
            else:
                send(col_send_a.at[n], col_mid.at[place], ca_send, ca_recv, at(yat(dy), z, core(k), x))
    for dx in range(NX):
        for k in range(NC):
            place = (NX - dx) % NX
            if (dx, k) == (0, 0):
                col_far[c, place] = col_send_f[0]
            else:
                send(col_send_f.at[dx], col_far.at[c, place], cf_send, cf_recv, at(y, z, core(k), xat(dx)))

    compute_a([last], last_a, True)
    for n, dy in enumerate(NEAR_DY):
        for k in range(NC):
            send(
                last_a.at[n], end_near.at[SEEN_AS[n] * NC + c], ea_send, ea_recv, at(yat(dy), zat(4), core(k), x)
            )

    def row_lse(m, s):
        v = (m + jnp.log2(jnp.maximum(s, 1.0))).T
        peak = jnp.max(v, axis=0, keepdims=True)
        return peak + jnp.log2(jnp.sum(jnp.exp2(v - peak), axis=0, keepdims=True))

    def merge(v):
        peak = jnp.maximum(jnp.maximum(v[0], v[1]), jnp.maximum(v[2], v[3]))
        return peak + jnp.log2(sum(jnp.exp2(p - peak) for p in v))

    for a in range(BLK_DEV):
        lse = row_lse(row_max[a], row_sum[a])
        for h in range(2):
            row_send[h, a:a + 1, :] = lse[:, h * 128:(h + 1) * 128]
    for dx in range(1, NX):
        xx = xat(dx)
        send(row_send.at[xx // 2], row_got.at[x], x_send, x_recv, at(y, z, c, xx))
    row_got[x] = row_send[x // 2]

    await_bytes(col_got.at[pl.ds(0, 5)], ca_recv)
    await_bytes(col_got.at[pl.ds(0, 7)], cf_recv)
    for cc in range(NC):
        col_mid[NEAR * NC + cc] = merge([col_far[cc, i] for i in range(NX)])
    for zz in range(NZ):
        for s in range(PLANE):
            col_turn[zz, s:s + 1, :] = col_mid[s, zz:zz + 1, :]
    for dz in (1, 2, 3, 5, 6, 7):
        zz = zat(dz)
        send(col_turn.at[zz], col_got.at[z], cz_send, cz_recv, at(y, zz, c, x))
    col_got[z] = col_turn[z]

    compute_f([last], last_f, True)
    for dx in range(NX):
        for k in range(NC):
            send(
                last_f.at[dx], end_far.at[c, (NX - dx) % NX], ef_send, ef_recv, at(y, zat(4), core(k), xat(dx))
            )
    for i in range(BLK_DEV // 2):
        m = far_max[2 * i:2 * i + 2].reshape(LANES, 128)
        s = far_sum[2 * i:2 * i + 2].reshape(LANES, 128)
        far_send[i:i + 1, :] = row_lse(m, s)
    send(far_send, far_got, x_send, x_recv, far_device)

    await_bytes(row_got, x_recv)
    await_bytes(col_turn.at[pl.ds(0, 6)], cz_recv)
    await_bytes(end_near, ea_recv)
    await_bytes(end_far, ef_recv)
    opposite = zat(4)
    for s in range(NEAR * NC):
        col_got[opposite, s:s + 1, :] = end_near[s, 0:1, :]
    for cc in range(NC):
        s = NEAR * NC + cc
        col_got[opposite, s:s + 1, :] = merge([end_far[cc, i, 0:1, :] for i in range(NX)])

    def to_front(v, shift_it):
        return jnp.where(shift_it, pltpu.roll(v, Q, 1), v)

    got = col_got[...].reshape(NZ * PLANE, 128)
    who = pcol[...].reshape(NZ * PLANE, 128)
    for b in range(BLK_DEV):
        is_it = who == b
        v = jnp.where(is_it, got, LOW)
        peak = jnp.max(v, axis=0, keepdims=True)
        total = jnp.sum(jnp.where(is_it, jnp.exp2(v - peak), 0.0), axis=0, keepdims=True)
        col_max[b:b + 1, 0:128] = peak
        col_sum[b:b + 1, 0:128] = total
        v = far_got[b // 2:b // 2 + 1, :]
        col_max[b:b + 1, 128:256] = v if b % 2 == 0 else pltpu.roll(v, Q, 1)
    col_peak = to_front(col_max[:, 0:128], c == 1)
    col_total = to_front(col_sum[:, 0:128], c == 1)
    rows = [to_front(row_got[i], lax.rem(x, 2) == 1) for i in range(NX)]
    rows.append(col_max[:, 128:256])
    peak = col_peak
    for r in rows:
        peak = jnp.maximum(peak, r)
    total = col_total * jnp.exp2(col_peak - peak)
    for r in rows:
        total += jnp.exp2(r - peak)
    result = peak + jnp.log2(total)
    out[...] = result[:BLK_DEV, :Q]
    await_bytes(held_a.at[pl.ds(0, 7)], z_send)
    await_bytes(q0, g_send)
    await_bytes(staged_a, a_send)
    await_bytes(staged_a, f_send)
    await_bytes(held_f.at[pl.ds(0, 2)], w_send)
    await_bytes(col_turn.at[pl.ds(0, 5)], ca_send)
    await_bytes(col_turn.at[pl.ds(0, 7)], cf_send)
    await_bytes(col_turn.at[pl.ds(0, 6)], cz_send)
    await_bytes(end_near, ea_send)
    await_bytes(end_far, ef_send)
    await_bytes(row_got, x_send)


def body(embeddings, pick, mask):
    vmem = pl.BlockSpec(memory_space=pltpu.VMEM)
    anywhere = pl.BlockSpec(memory_space=pl.ANY)
    dma = pltpu.SemaphoreType.DMA
    f32, bf16 = jnp.float32, jnp.bfloat16
    slab = pltpu.VMEM((BLK_DEV, Q, W), bf16)
    base2 = pl.pallas_call(
        kernel,
        out_shape=jax.ShapeDtypeStruct((BLK_DEV, Q), f32),
        in_specs=[anywhere, anywhere, anywhere],
        out_specs=vmem,
        scratch_shapes=[
            pltpu.SMEM((64, 64), jnp.int32),
            slab,
            *[pltpu.VMEM((BLK_DEV, Q // 2, W), bf16)] * 12,
            *[pltpu.VMEM((BLK_DEV, Q // 4, W), bf16)] * 4,
            slab,
            pltpu.VMEM((BLK_DEV, BR, W), bf16),
            pltpu.VMEM((NZ, NEAR * NC - 1, Q, W), bf16),
            pltpu.VMEM((NZ, Q, W), bf16),
            pltpu.VMEM((NZ, NEAR * NC, Q, W), bf16),
            pltpu.VMEM((NZ, NX * NC, Q, W), bf16),
            pltpu.VMEM((BLK_DEV, 64, 64), jnp.int32),
            pltpu.VMEM((2, 8, 128), f32),
            pltpu.VMEM((NZ, 8, COLS_A), f32),
            pltpu.VMEM((NZ, 8, COLS_F), f32),
            pltpu.VMEM((NZ, PLANE, 128), jnp.int32),
            pltpu.VMEM((BLK_DEV, BR, 128), f32),
            pltpu.VMEM((BLK_DEV, BR, 128), f32),
            pltpu.VMEM((BLK_DEV, Q, 128), f32),
            pltpu.VMEM((BLK_DEV, Q, 128), f32),
            pltpu.VMEM((2, BR, 2 * COLS_A), f32),
            pltpu.VMEM((2, 2 * Q, 2 * COLS_F), f32),
            pltpu.VMEM((8, 2 * COLS_F), f32),
            pltpu.VMEM((8, 2 * COLS_F), f32),
            pltpu.VMEM((NEAR, NZ, 128), f32),
            pltpu.VMEM((NX, NZ, 128), f32),
            pltpu.VMEM((PLANE, NZ, 128), f32),
            pltpu.VMEM((NC, NX, NZ, 128), f32),
            pltpu.VMEM((NZ, PLANE, 128), f32),
            pltpu.VMEM((NZ, PLANE, 128), f32),
            pltpu.VMEM((2, 8, 128), f32),
            pltpu.VMEM((NX, 8, 128), f32),
            pltpu.VMEM((8, 128), f32),
            pltpu.VMEM((8, 128), f32),
            pltpu.VMEM((NEAR, 8, 128), f32),
            pltpu.VMEM((NX, 8, 128), f32),
            pltpu.VMEM((NEAR * NC, 8, 128), f32),
            pltpu.VMEM((NC, NX, 8, 128), f32),
            dma((4,)),
            dma, dma((4, 2)),
            dma, dma,
            dma, dma((NZ,)),
            dma, dma((NZ + 1, 2)),
            dma, dma((NZ,)),
            *[dma] * 12,
        ],
        compiler_params=pltpu.CompilerParams(
            collective_id=0, has_side_effects=True, vmem_limit_bytes=56 * 1024 * 1024
        ),
        cost_estimate=pl.CostEstimate(
            flops=2 * 1536 * 4096 * W, bytes_accessed=8 * 1024 * 1024, transcendentals=2 * 1536 * 4096
        ),
    )(embeddings.reshape(BLK_DEV, BR, W), pick, mask.transpose(2, 0, 1))
    return base2 * LN2


def solution(mesh):
    return jax.shard_map(
        body,
        mesh=mesh,
        in_specs=(P("blk", None), P(), P()),
        out_specs=P("blk", "rep"),
        check_vma=False,
    )
```
